32 devices in a mesh: dst: 8 (over y, x, core), src: 4 (over z).
Axes of the slice: x: 2, y: 2, z: 4, core: 2. Of those that a mesh axis runs over, the one named last changes fastest.
Arguments:
- features: bfloat16 [3072, 768], P(('src', 'dst')), may hold values from -6 to 6
- relation_weight: bfloat16 [768, 3, 256], replicated, may hold values from -0.21875 to 0.21875
- bias: bfloat16 [256], replicated, may hold values from -3 to 3
- block_values: bfloat16 [8, 4, 3, 16, 128, 128], P('dst', 'src'), may hold values from 0 to 0.06591797
- block_list: int32 [8, 4, 3, 16], P('dst', 'src'), may hold values from 0 to 17, as said below
- block_count: int32 [8, 4, 3], P('dst', 'src'), may hold values from 4 to 16, as said below
- cotangent: bfloat16 [3072, 256], P(('dst', 'src')), may hold values from -6 to 6
Outputs:
- output: bfloat16 [3072, 256], P(('dst', 'src'))
- weight_grad: float32 [768, 3, 256], replicated
- bias_grad: float32 [256], replicated
The draws below stay inside these ranges and needn't reach their ends.
Inputs may be any that keep to these rules, and one draw needn't show every extreme that they name: `block_list`: within one tile and relation the 16 slots name different blocks. `block_count`: some tile and relation fills all 16 slots.
All inputs are finite; a program needn't handle non-finite values.
Results may differ from the reference program's by a relative error of at most 0.0075.
Values may be sent and summed in bfloat16 or wider, within the bound.
No kernel may reach another device: no remote copies, remote signals or barrier semaphores. Data moves between devices by JAX's collectives and lax.ppermute only.
A program may use at most 64 MiB of HBM per device.

```python
import jax
import jax.numpy as jnp
from jax import lax

D = 768
HID = 256
RELS = 3
BS = 128
MAXB = 16
DROWS = 384
NODES = 3072
TCOLS = 768
N_DST = 8
N_SRC = 4


def draw_block_list(key, part):
    total_blocks = DROWS // BS * (TCOLS // BS)
    tile_keys = jax.random.split(key, N_DST * N_SRC * RELS)

    def one_list(tile_key):
        return jax.random.permutation(tile_key, total_blocks)[:MAXB]
    lists = jax.vmap(one_list)(tile_keys)
    return lists.reshape(N_DST, N_SRC, RELS, MAXB).astype(jnp.int32)


def draw_block_count(key, part):
    counts = jax.random.randint(key, (N_DST * N_SRC * RELS,), MAXB // 4, MAXB + 1)
    target = jax.random.randint(jax.random.fold_in(key, 7), (), 0, N_DST * N_SRC * RELS)
    positions = jnp.arange(N_DST * N_SRC * RELS)
    counts = jnp.where(positions == target, MAXB, counts)
    return counts.reshape(N_DST, N_SRC, RELS).astype(jnp.int32)


def block_scale(rng, dims, pieces, least, largest):
    def one(axis_at, shards_of):
        steps = jax.random.uniform(jax.random.fold_in(jax.random.fold_in(rng, 6), axis_at), (shards_of,), jnp.float32, least / len(pieces), largest / len(pieces))
        return jnp.repeat(jnp.exp(steps), dims[axis_at] // shards_of).reshape((-1,) + (1,) * (len(dims) - axis_at - 1))

    loudness = one(*pieces[0])
    for cut in pieces[1:]:
        loudness = loudness * one(*cut)
    return loudness


def normal_values(own_key, shape, scale, most, pieces=(), held_as=jnp.bfloat16):
    loudness = block_scale(own_key, shape, pieces, -0.22, 0.18) if pieces else 1.0
    values = jax.random.normal(own_key, shape, jnp.float32) * scale * loudness
    return jnp.minimum(jnp.maximum(values, -most), most).astype(held_as)


def setup_inputs(seed: int = 0) -> dict:
    streams_of = jax.random.split(jax.random.key(seed), 8)
    features = normal_values(streams_of[0], (NODES, D), 1.0, 6.0, ((0, 32),))
    relation_weight = normal_values(streams_of[1], (D, RELS, HID), D ** -0.5, 0.21875)
    bias = normal_values(streams_of[2], (HID,), 0.5, 3.0)
    block_values = jnp.clip(0.06591797 * jax.random.uniform(streams_of[3], (N_DST, N_SRC, RELS, MAXB, BS, BS), jnp.float32) ** block_scale(streams_of[3], (N_DST, N_SRC, RELS, MAXB, BS, BS), ((0, 8), (1, 4)), -0.2, 0.2), 0.0, 0.06591797).astype(jnp.bfloat16)
    block_list = draw_block_list(jax.random.fold_in(streams_of[7], 71), 0)
    block_count = draw_block_count(jax.random.fold_in(streams_of[7], 71), 0)
    cotangent = normal_values(streams_of[6], (NODES, HID), 1.0, 6.0, ((0, 32),))
    return {"features": features, "relation_weight": relation_weight, "bias": bias, "block_values": block_values, "block_list": block_list, "block_count": block_count, "cotangent": cotangent}


def reference(features, relation_weight, bias, block_values, block_list, block_count, cotangent):
    blocks_across = TCOLS // BS
    blocks_down = DROWS // BS
    slot_iota = jnp.arange(MAXB).astype(jnp.int32)
    live = (slot_iota[None, None, None, :] < block_count[..., None]).astype(jnp.float32)
    projected = jnp.dot(features, relation_weight.reshape(D, RELS * HID), preferred_element_type=jnp.float32)
    projected = projected.astype(jnp.bfloat16).reshape(N_SRC, blocks_across, BS, RELS, HID)
    feature_blocks = features.reshape(N_SRC, blocks_across, BS, D)
    source_index = jnp.arange(N_SRC).astype(jnp.int32)[:, None, None]
    relation_index = jnp.arange(RELS).astype(jnp.int32)[None, :, None]
    down_iota = jnp.arange(blocks_down).astype(jnp.int32)

    def band_parts(band):
        weighted = block_values[band].astype(jnp.float32) * live[band][..., None, None]
        column = block_list[band] % blocks_across
        row_index = block_list[band] // blocks_across
        onehot = (row_index[..., None] == down_iota).astype(jnp.float32)
        return weighted, column, row_index, onehot

    def band_message(band):
        weighted, column, row_index, onehot = band_parts(band)
        picked = projected[source_index, column, :, relation_index, :].astype(jnp.float32)
        blockwise = jnp.einsum("srbij,srbjh->srbih", weighted, picked, precision=lax.Precision.HIGHEST)
        banded = jnp.einsum("srbq,srbih->qih", onehot, blockwise, precision=lax.Precision.HIGHEST)
        return banded.reshape(DROWS, HID)

    message = lax.map(band_message, jnp.arange(N_DST).astype(jnp.int32)).reshape(NODES, HID)
    pre = message + bias.astype(jnp.float32)
    sigma = jax.nn.sigmoid(pre)
    output = (pre * sigma).astype(jnp.bfloat16)
    grad_pre = (cotangent.astype(jnp.float32) * sigma * (1.0 + pre * (1.0 - sigma))).astype(jnp.bfloat16)
    grad_float = grad_pre.astype(jnp.float32)
    bias_grad = jnp.sum(grad_float, axis=0)
    grad_bands = grad_float.reshape(N_DST, DROWS, HID)

    def band_back(accumulated, band):
        weighted, column, row_index, onehot = band_parts(band)
        picked = feature_blocks[source_index, column].astype(jnp.float32)
        blockwise = jnp.einsum("srbij,srbjd->srbid", weighted, picked, precision=lax.Precision.HIGHEST)
        tiles = jnp.einsum("srbq,srbid->srqid", onehot, blockwise, precision=lax.Precision.HIGHEST)
        tiles = lax.optimization_barrier(tiles.reshape(N_SRC, RELS, DROWS, D).astype(jnp.bfloat16))
        tiles = tiles.astype(jnp.float32)
        contribution = jnp.einsum("srnd,nh->drh", tiles, grad_bands[band], precision=lax.Precision.HIGHEST)
        return accumulated + contribution, None

    start = jnp.zeros((D, RELS, HID), jnp.float32)
    weight_grad, unused = lax.scan(band_back, start, jnp.arange(N_DST).astype(jnp.int32))
    return output, weight_grad, bias_grad
```

```python
import functools

import jax
import jax.numpy as jnp
from jax import lax
from jax.experimental import pallas as pl
from jax.experimental.pallas import tpu as pltpu
from jax.sharding import PartitionSpec as P

BF = jnp.bfloat16
F32 = jnp.float32
TAIL = 16
ANY = pl.BlockSpec(memory_space=pl.ANY)
SMEM = pl.BlockSpec(memory_space=pltpu.SMEM)
VMEM = pl.BlockSpec(memory_space=pltpu.VMEM)


def shape(dims, dtype):
    return jax.ShapeDtypeStruct(dims, dtype)


def call(body, out, specs, *args, scratch=(), flops=0, moved=0, aliases=None):
    return pl.pallas_call(
        body,
        out_shape=out,
        in_specs=list(specs),
        out_specs=jax.tree.map(lambda _: VMEM, out),
        scratch_shapes=list(scratch),
        input_output_aliases=aliases or {},
        compiler_params=pltpu.CompilerParams(vmem_limit_bytes=24 * 2**20),
        cost_estimate=pl.CostEstimate(flops=flops, bytes_accessed=moved, transcendentals=0),
    )(*args)


def assemble(band_rows, list_ref, count_ref, values_ref, dense_ref):
    slots = values_ref.shape[0] // count_ref.shape[0]
    size = values_ref.shape[1]
    across = dense_ref.shape[1] // size
    dense_ref[...] = jnp.zeros_like(dense_ref)

    def place(at, carry):
        relation = lax.div(at, slots)

        @pl.when(lax.rem(at, slots) < count_ref[relation])
        def _():
            k = list_ref[at]
            row = pl.multiple_of(relation * band_rows + lax.div(k, across) * size, size)
            column = pl.multiple_of(lax.rem(k, across) * size, size)
            dense_ref[pl.ds(row, size), pl.ds(column, size)] = values_ref[at]

        return carry

    lax.fori_loop(0, values_ref.shape[0], place, 0)


def forward(n_src, count, where_ref, dense_ref, weight_ref, *refs):
    pieces = refs[:count]
    tile_ref, own_ref = refs[count : count + 2]
    sends = refs[count + 2 : count + 1 + n_src]
    features, message, sems = refs[count + 1 + n_src :]
    rows = pieces[0].shape[0]
    copies = []
    for i, piece in enumerate(pieces):
        start = pl.multiple_of(where_ref[1 + i] * rows, 16)
        copies.append(pltpu.make_async_copy(piece, features.at[pl.ds(start, rows)], sems.at[i]))
        copies[-1].start()
    for copy in copies:
        copy.wait()
    width = features.shape[1]
    band_rows = tile_ref.shape[0]
    total = None
    for r in range(dense_ref.shape[0] // band_rows):
        part = jnp.dot(
            dense_ref[r * band_rows : (r + 1) * band_rows],
            features[...],
            preferred_element_type=F32,
        ).astype(BF)
        tile_ref[:, r * width : (r + 1) * width] = part
        term = jnp.dot(
            part, weight_ref[r * width : (r + 1) * width], preferred_element_type=F32
        )
        total = term if total is None else total + term
    message[...] = total
    block = own_ref.shape[0]
    for m in range(n_src):
        start = pl.multiple_of((where_ref[0] ^ m) * block, 16)
        mine = message[pl.ds(start, block)]
        if m == 0:
            own_ref[...] = mine
        else:
            sends[m - 1][...] = mine.astype(BF)


def transpose(tile_ref, out_ref):
    step = 256
    for at in range(0, tile_ref.shape[1], step):
        out_ref[at : at + step] = tile_ref[:, at : at + step].T


def activate(bias_ref, cotangent_ref, own_ref, *refs):
    *others, output_ref, grad_ref = refs
    pre = own_ref[...]
    for other in others:
        pre = pre + other[...].astype(F32)
    pre = pre + bias_ref[...].astype(F32)
    sigma = jax.nn.sigmoid(pre)
    output_ref[...] = (pre * sigma).astype(BF)
    grad_ref[...] = (
        cotangent_ref[...].astype(F32) * sigma * (1.0 + pre * (1.0 - sigma))
    ).astype(BF)


def split_row(row):
    at = lax.broadcasted_iota(jnp.int32, (TAIL, row.shape[1]), 0)
    high = row.astype(BF).astype(F32)
    return jnp.where(at == 0, high, jnp.where(at == 1, row - high, 0.0)).astype(BF)


def join_row(tail):
    return jnp.sum(tail.astype(F32), axis=0, keepdims=True)


def backward(n_src, chips, where_ref, tile_ref, *refs):
    grads = refs[:n_src]
    keep_ref, send_ref, bias_ref, grad = refs[n_src:]
    block = grads[0].shape[0]
    for m in range(n_src):
        start = pl.multiple_of((where_ref[0] ^ m) * block, 16)
        grad[pl.ds(start, block)] = grads[m][...]
    piece = keep_ref.shape[0] // chips
    half = tile_ref.shape[0] // 2
    bias = jnp.sum(grad[...].astype(F32), axis=0, keepdims=True)
    tail = split_row(bias)
    bias_ref[...] = jnp.broadcast_to(join_row(tail), bias_ref.shape)
    send_ref[pl.ds(piece * chips, TAIL)] = tail
    for ref, core in ((send_ref, 1 - where_ref[1]), (keep_ref, where_ref[1])):
        for m in range(chips):
            start = pl.multiple_of(core * half + (where_ref[2] ^ m) * piece, 16)
            ref[m * piece : (m + 1) * piece] = jnp.dot(
                tile_ref[pl.ds(start, piece)], grad[...], preferred_element_type=F32
            ).astype(ref.dtype)


def add_cores(chips, keep_ref, bias_ref, received_ref, own_ref, total_ref, *sends):
    piece = own_ref.shape[0]
    tail = split_row(bias_ref[0:1] + join_row(received_ref[pl.ds(piece * chips, TAIL)]))
    total_ref[...] = jnp.broadcast_to(join_row(tail), total_ref.shape)
    for m in range(chips):
        at = pl.ds(m * piece, piece)
        both = keep_ref[at] + received_ref[at].astype(F32)
        if m == 0:
            own_ref[...] = both
        else:
            sends[m - 1][0:piece] = both.astype(BF)
            sends[m - 1][piece : piece + TAIL] = tail


def tree(terms):
    while len(terms) > 1:
        terms = [a + b for a, b in zip(terms[::2], terms[1::2])]
    return terms[0]


def add_chips(own_ref, bias_ref, *refs):
    *received, sum_ref, total_ref = refs
    piece = own_ref.shape[0]
    tails = [join_row(other[pl.ds(piece, TAIL)]) for other in received]
    total_ref[...] = tree([bias_ref[0:1]] + tails)
    parts = [other[0:piece].astype(F32) for other in received]
    sum_ref[...] = tree([own_ref[...]] + parts).astype(BF)


def add_bands(*refs):
    *parts, out_ref = refs
    out_ref[...] = tree([part[...].astype(F32) for part in parts]).astype(BF)


def spread(chips, where_ref, *refs):
    *pieces, out_ref = refs
    rows = pieces[0].shape[0]
    half = out_ref.shape[0] // 2
    for i, piece in enumerate(pieces):
        core = where_ref[1] if i < chips else 1 - where_ref[1]
        start = core * half + (where_ref[2] ^ (i % chips)) * rows
        out_ref[pl.ds(pl.multiple_of(start, 16), rows)] = piece[...].astype(F32)


def swap(x, axis, n, mask):
    return lax.ppermute(x, axis, [(i, i ^ mask) for i in range(n)])


def on_device(features, relation_weight, bias, block_values, block_list, block_count, cotangent):
    n_dst, n_src = lax.axis_size("dst"), lax.axis_size("src")
    own_rows, width = features.shape
    relations, hidden = relation_weight.shape[1:]
    block_size = block_values.shape[5]
    tile_columns = own_rows * n_dst
    block = cotangent.shape[0]
    band_rows = block * n_src
    weight = relation_weight.transpose(1, 0, 2).reshape(relations * width, hidden)
    dense = call(
        functools.partial(assemble, band_rows),
        shape((relations * band_rows, tile_columns), BF),
        (SMEM, SMEM, VMEM),
        block_list.reshape(-1),
        block_count.reshape(-1),
        block_values.reshape(-1, block_size, block_size),
        flops=10**8,
        moved=4 * 2**20,
    )
    if n_dst == 8 and n_src == 4 and (relations * width) % (8 * 16) == 0:
        return few_devices(features, weight, bias, dense, cotangent, relations)
    gathered = lax.all_gather(features, "dst", axis=0, tiled=True)
    tile = jnp.dot(dense, gathered, preferred_element_type=F32).astype(BF)
    tile = tile.reshape(relations, band_rows, width)
    partial = jnp.einsum(
        "rnd,rdh->nh",
        tile,
        weight.reshape(relations, width, hidden),
        preferred_element_type=F32,
    )
    pre = lax.psum_scatter(partial, "src", scatter_dimension=0, tiled=True)
    pre = pre + bias.astype(F32)
    sigma = jax.nn.sigmoid(pre)
    output = (pre * sigma).astype(BF)
    grad = (cotangent.astype(F32) * sigma * (1.0 + pre * (1.0 - sigma))).astype(BF)
    band_grad = lax.all_gather(grad, "src", axis=0, tiled=True)
    weight_term = jnp.einsum("rnd,nh->rdh", tile, band_grad, preferred_element_type=F32)
    weight_grad, bias_grad = lax.psum(
        (weight_term, jnp.sum(grad.astype(F32), axis=0)), ("dst", "src")
    )
    return output, weight_grad.transpose(1, 0, 2), bias_grad


def few_devices(features, weight, bias, dense, cotangent, relations):
    n_dst, n_src = lax.axis_size("dst"), lax.axis_size("src")
    chips = n_dst // 2
    own_rows, width = features.shape
    block, hidden = cotangent.shape
    band_rows = block * n_src
    total_rows = weight.shape[0]
    piece = total_rows // n_dst
    me, z = lax.axis_index("dst"), lax.axis_index("src")
    place = jnp.stack([z, me % 2, me // 2]).astype(jnp.int32)

    def over_chips(x, m):
        return swap(x, "dst", n_dst, 2 * m)

    def over_core(x):
        return swap(x, "dst", n_dst, 1)

    def over_src(x, m):
        return swap(x, "src", n_src, m)

    near = [features] + [over_chips(features, m) for m in range(1, chips)]
    far = [over_core(x) for x in near]
    order = [me ^ (2 * m) for m in range(chips)] + [me ^ (2 * m + 1) for m in range(chips)]
    where = jnp.stack([z] + order).astype(jnp.int32)
    tile, own, *sends = call(
        functools.partial(forward, n_src, n_dst),
        [shape((band_rows, relations * width), BF), shape((block, hidden), F32)]
        + [shape((block, hidden), BF)] * (n_src - 1),
        [SMEM, VMEM, VMEM] + [ANY] * n_dst,
        where,
        dense,
        weight,
        *near,
        *far,
        scratch=[
            pltpu.VMEM((own_rows * n_dst, width), BF),
            pltpu.VMEM((band_rows, hidden), F32),
            pltpu.SemaphoreType.DMA((n_dst,)),
        ],
        flops=2 * 10**9,
        moved=8 * 2**20,
    )
    received = [over_src(x, m + 1) for m, x in enumerate(sends)]
    turned = call(
        transpose,
        shape((total_rows, band_rows), BF),
        [VMEM],
        tile,
        flops=10**8,
        moved=4 * 2**20,
    )
    output, grad = call(
        activate,
        [shape((block, hidden), BF)] * 2,
        [VMEM] * (3 + len(received)),
        bias.reshape(1, hidden),
        cotangent,
        own,
        *received,
    )
    grads = [grad] + [over_src(grad, m) for m in range(1, n_src)]
    keep, send, bias_part = call(
        functools.partial(backward, n_src, chips),
        [
            shape((piece * chips, hidden), F32),
            shape((piece * chips + TAIL, hidden), BF),
            shape((8, hidden), F32),
        ],
        [SMEM, VMEM] + [VMEM] * n_src,
        place,
        turned,
        *grads,
        scratch=[pltpu.VMEM((band_rows, hidden), BF)],
    )
    own, bias_part, *sends = call(
        functools.partial(add_cores, chips),
        [shape((piece, hidden), F32), shape((8, hidden), F32)]
        + [shape((piece + TAIL, hidden), BF)] * (chips - 1),
        [VMEM] * 3,
        keep,
        bias_part,
        over_core(send),
    )
    received = [over_chips(x, m + 1) for m, x in enumerate(sends)]
    part, bias_grad = call(
        add_chips,
        [shape((piece, hidden), BF), shape((1, hidden), F32)],
        [VMEM] * (1 + chips),
        own,
        bias_part,
        *received,
    )
    parts = [part] + [over_src(part, m) for m in range(1, n_src)]
    chunk = call(add_bands, shape((piece, hidden), BF), [VMEM] * n_src, *parts)
    near = [chunk] + [over_chips(chunk, m) for m in range(1, chips)]
    far = [over_core(x) for x in near]
    weight_grad = call(
        functools.partial(spread, chips),
        shape((total_rows, hidden), F32),
        [SMEM] + [VMEM] * n_dst,
        place,
        *near,
        *far,
    )
    weight_grad = weight_grad.reshape(relations, width, hidden).transpose(1, 0, 2)
    return output, weight_grad, bias_grad.reshape(hidden)


def solution(mesh):
    in_specs = (
        P(("src", "dst"), None),
        P(),
        P(),
        P("dst", "src", None, None, None, None),
        P("dst", "src", None, None),
        P("dst", "src", None),
        P(("dst", "src"), None),
    )
    out_specs = (P(("dst", "src"), None), P(), P())
    return jax.shard_map(
        on_device, mesh=mesh, in_specs=in_specs, out_specs=out_specs, check_vma=False
    )
```

```python
import functools

import jax
import jax.numpy as jnp
from jax import lax
from jax.experimental import pallas as pl
from jax.experimental.pallas import tpu as pltpu
from jax.sharding import PartitionSpec as P

BF = jnp.bfloat16
F32 = jnp.float32
TAIL = 16
ANY = pl.BlockSpec(memory_space=pl.ANY)
SMEM = pl.BlockSpec(memory_space=pltpu.SMEM)
VMEM = pl.BlockSpec(memory_space=pltpu.VMEM)


def shape(dims, dtype):
    return jax.ShapeDtypeStruct(dims, dtype)


def call(body, out, specs, *args, scratch=(), flops=0, moved=0, aliases=None, out_spec=VMEM):
    return pl.pallas_call(
        body,
        out_shape=out,
        in_specs=list(specs),
        out_specs=jax.tree.map(lambda _: out_spec, out),
        scratch_shapes=list(scratch),
        input_output_aliases=aliases or {},
        compiler_params=pltpu.CompilerParams(vmem_limit_bytes=24 * 2**20),
        cost_estimate=pl.CostEstimate(flops=flops, bytes_accessed=moved, transcendentals=0),
    )(*args)


def assemble(band_rows, list_ref, count_ref, values_ref, dense_ref):
    slots = values_ref.shape[0] // count_ref.shape[0]
    size = values_ref.shape[1]
    across = dense_ref.shape[1] // size
    dense_ref[...] = jnp.zeros_like(dense_ref)

    def place(at, carry):
        relation = lax.div(at, slots)

        @pl.when(lax.rem(at, slots) < count_ref[relation])
        def _():
            k = list_ref[relation, lax.rem(at, slots)]
            row = pl.multiple_of(relation * band_rows + lax.div(k, across) * size, size)
            column = pl.multiple_of(lax.rem(k, across) * size, size)
            dense_ref[pl.ds(row, size), pl.ds(column, size)] = values_ref[at]

        return carry

    lax.fori_loop(0, values_ref.shape[0], place, 0)


def forward(n_src, count, where_ref, dense_ref, weight_ref, *refs):
    pieces = refs[:count]
    tile_ref, own_ref = refs[count : count + 2]
    sends = refs[count + 2 : count + 1 + n_src]
    features, message = refs[count + 1 + n_src :]
    rows = pieces[0].shape[0]
    for i, piece in enumerate(pieces):
        start = pl.multiple_of(where_ref[1 + i] * rows, 16)
        features[pl.ds(start, rows)] = piece[...]
    width = features.shape[1]
    band_rows = tile_ref.shape[0]
    step = 128
    for i in range(0, band_rows, step):
        for r in range(dense_ref.shape[0] // band_rows):
            tile_ref[i : i + step, r * width : (r + 1) * width] = jnp.dot(
                dense_ref[r * band_rows + i : r * band_rows + i + step],
                features[...],
                preferred_element_type=F32,
            ).astype(BF)
    message[...] = jnp.dot(tile_ref[...], weight_ref[...], preferred_element_type=F32)
    block = own_ref.shape[0]
    for m in range(n_src):
        start = pl.multiple_of((where_ref[0] ^ m) * block, 16)
        mine = message[pl.ds(start, block)]
        if m == 0:
            own_ref[...] = mine
        else:
            sends[m - 1][...] = mine.astype(BF)


def transpose(tile_ref, out_ref):
    step = 256
    for at in range(0, tile_ref.shape[1], step):
        out_ref[at : at + step] = tile_ref[:, at : at + step].T


def activate(bias_ref, cotangent_ref, own_ref, *refs):
    *others, output_ref, grad_ref = refs
    pre = own_ref[...]
    for other in others:
        pre = pre + other[...].astype(F32)
    pre = pre + bias_ref[...].astype(F32)
    sigma = jax.nn.sigmoid(pre)
    output_ref[...] = (pre * sigma).astype(BF)
    grad_ref[...] = (
        cotangent_ref[...].astype(F32) * sigma * (1.0 + pre * (1.0 - sigma))
    ).astype(BF)


def split_row(row):
    at = lax.broadcasted_iota(jnp.int32, (TAIL, row.shape[1]), 0)
    high = row.astype(BF).astype(F32)
    return jnp.where(at == 0, high, jnp.where(at == 1, row - high, 0.0)).astype(BF)


def join_row(tail):
    return jnp.sum(tail.astype(F32), axis=0, keepdims=True)


def backward(n_src, chips, where_ref, tile_ref, *refs):
    grads = refs[:n_src]
    keep_ref, send_ref, bias_ref, grad = refs[n_src:]
    block = grads[0].shape[0]
    for m in range(n_src):
        start = pl.multiple_of((where_ref[0] ^ m) * block, 16)
        grad[pl.ds(start, block)] = grads[m][...]
    piece = keep_ref.shape[0] // chips
    half = tile_ref.shape[0] // 2
    bias = jnp.sum(grad[...].astype(F32), axis=0, keepdims=True)
    tail = split_row(bias)
    bias_ref[...] = jnp.broadcast_to(join_row(tail), bias_ref.shape)
    send_ref[pl.ds(piece * chips, TAIL)] = tail
    for ref, core in ((send_ref, 1 - where_ref[1]), (keep_ref, where_ref[1])):
        for m in range(chips):
            start = pl.multiple_of(core * half + (where_ref[2] ^ m) * piece, 16)
            ref[m * piece : (m + 1) * piece] = jnp.dot(
                tile_ref[pl.ds(start, piece)], grad[...], preferred_element_type=F32
            ).astype(ref.dtype)


def add_cores(chips, keep_ref, bias_ref, received_ref, own_ref, total_ref, *sends):
    piece = own_ref.shape[0]
    tail = split_row(bias_ref[0:1] + join_row(received_ref[pl.ds(piece * chips, TAIL)]))
    total_ref[...] = jnp.broadcast_to(join_row(tail), total_ref.shape)
    for m in range(chips):
        at = pl.ds(m * piece, piece)
        both = keep_ref[at] + received_ref[at].astype(F32)
        if m == 0:
            own_ref[...] = both
        else:
            sends[m - 1][0:piece] = both.astype(BF)
            sends[m - 1][piece : piece + TAIL] = tail


def tree(terms):
    while len(terms) > 1:
        terms = [a + b for a, b in zip(terms[::2], terms[1::2])]
    return terms[0]


def add_chips(own_ref, bias_ref, *refs):
    *received, sum_ref, total_ref = refs
    piece = own_ref.shape[0]
    tails = [join_row(other[pl.ds(piece, TAIL)]) for other in received]
    total_ref[...] = tree([bias_ref[0:1]] + tails)
    parts = [other[0:piece].astype(F32) for other in received]
    sum_ref[...] = tree([own_ref[...]] + parts).astype(BF)


def add_bands(*refs):
    *parts, out_ref = refs
    out_ref[...] = tree([part[...].astype(F32) for part in parts]).astype(BF)


def spread(which, where_ref, *refs):
    chunks, (out_ref, wide, sems) = refs[: len(which)], refs[-3:]
    rows = chunks[0].shape[0]
    half = out_ref.shape[0] // 2
    copies = []
    for i, (core, chip) in enumerate(which):
        wide[i] = chunks[i][...].astype(F32)
        start = (where_ref[1] ^ core) * half + (where_ref[2] ^ chip) * rows
        target = out_ref.at[pl.ds(pl.multiple_of(start, 16), rows)]
        copies.append(pltpu.make_async_copy(wide.at[i], target, sems.at[i]))
        copies[-1].start()
    for copy in copies:
        copy.wait()


def swap(x, axis, n, mask):
    return lax.ppermute(x, axis, [(i, i ^ mask) for i in range(n)])


def on_device(features, relation_weight, bias, block_values, block_list, block_count, cotangent):
    n_dst, n_src = lax.axis_size("dst"), lax.axis_size("src")
    own_rows, width = features.shape
    relations, hidden = relation_weight.shape[1:]
    block_size = block_values.shape[5]
    tile_columns = own_rows * n_dst
    block = cotangent.shape[0]
    band_rows = block * n_src
    weight = relation_weight.transpose(1, 0, 2).reshape(relations * width, hidden)
    dense = call(
        functools.partial(assemble, band_rows),
        shape((relations * band_rows, tile_columns), BF),
        (SMEM, SMEM, VMEM),
        block_list.reshape(relations, -1),
        block_count.reshape(-1),
        block_values.reshape(-1, block_size, block_size),
        flops=10**8,
        moved=4 * 2**20,
    )
    if n_dst == 8 and n_src == 4 and (relations * width) % (8 * 16) == 0:
        return few_devices(features, weight, bias, dense, cotangent, relations)
    gathered = lax.all_gather(features, "dst", axis=0, tiled=True)
    tile = jnp.dot(dense, gathered, preferred_element_type=F32).astype(BF)
    tile = tile.reshape(relations, band_rows, width)
    partial = jnp.einsum(
        "rnd,rdh->nh",
        tile,
        weight.reshape(relations, width, hidden),
        preferred_element_type=F32,
    )
    pre = lax.psum_scatter(partial, "src", scatter_dimension=0, tiled=True)
    pre = pre + bias.astype(F32)
    sigma = jax.nn.sigmoid(pre)
    output = (pre * sigma).astype(BF)
    grad = (cotangent.astype(F32) * sigma * (1.0 + pre * (1.0 - sigma))).astype(BF)
    band_grad = lax.all_gather(grad, "src", axis=0, tiled=True)
    weight_term = jnp.einsum("rnd,nh->rdh", tile, band_grad, preferred_element_type=F32)
    weight_grad, bias_grad = lax.psum(
        (weight_term, jnp.sum(grad.astype(F32), axis=0)), ("dst", "src")
    )
    return output, weight_grad.transpose(1, 0, 2), bias_grad


def few_devices(features, weight, bias, dense, cotangent, relations):
    n_dst, n_src = lax.axis_size("dst"), lax.axis_size("src")
    chips = n_dst // 2
    own_rows, width = features.shape
    block, hidden = cotangent.shape
    band_rows = block * n_src
    total_rows = weight.shape[0]
    piece = total_rows // n_dst
    me, z = lax.axis_index("dst"), lax.axis_index("src")
    place = jnp.stack([z, me % 2, me // 2]).astype(jnp.int32)

    def over_chips(x, m):
        return swap(x, "dst", n_dst, 2 * m)

    def over_core(x):
        return swap(x, "dst", n_dst, 1)

    def over_src(x, m):
        return swap(x, "src", n_src, m)

    near = [features] + [over_chips(features, m) for m in range(1, chips)]
    near[1], dense = lax.optimization_barrier((near[1], dense))
    far = [over_core(x) for x in near]
    order = [me ^ (2 * m) for m in range(chips)] + [me ^ (2 * m + 1) for m in range(chips)]
    where = jnp.stack([z] + order).astype(jnp.int32)
    tile, own, *sends = call(
        functools.partial(forward, n_src, n_dst),
        [shape((band_rows, relations * width), BF), shape((block, hidden), F32)]
        + [shape((block, hidden), BF)] * (n_src - 1),
        [SMEM] + [VMEM] * (2 + n_dst),
        where,
        dense,
        weight,
        *near,
        *far,
        scratch=[
            pltpu.VMEM((own_rows * n_dst, width), BF),
            pltpu.VMEM((band_rows, hidden), F32),
        ],
        flops=2 * 10**9,
        moved=8 * 2**20,
    )
    received = [over_src(x, m + 1) for m, x in enumerate(sends)]
    turned = call(
        transpose,
        shape((total_rows, band_rows), BF),
        [VMEM],
        tile,
        flops=10**8,
        moved=4 * 2**20,
    )
    output, grad = call(
        activate,
        [shape((block, hidden), BF)] * 2,
        [VMEM] * (3 + len(received)),
        bias.reshape(1, hidden),
        cotangent,
        own,
        *received,
    )
    grads = [grad] + [over_src(grad, m) for m in range(1, n_src)]
    keep, send, bias_part = call(
        functools.partial(backward, n_src, chips),
        [
            shape((piece * chips, hidden), F32),
            shape((piece * chips + TAIL, hidden), BF),
            shape((8, hidden), F32),
        ],
        [SMEM, VMEM] + [VMEM] * n_src,
        place,
        turned,
        *grads,
        scratch=[pltpu.VMEM((band_rows, hidden), BF)],
    )
    own, bias_part, *sends = call(
        functools.partial(add_cores, chips),
        [shape((piece, hidden), F32), shape((8, hidden), F32)]
        + [shape((piece + TAIL, hidden), BF)] * (chips - 1),
        [VMEM] * 3,
        keep,
        bias_part,
        over_core(send),
    )
    received = [over_chips(x, m + 1) for m, x in enumerate(sends)]
    part, bias_grad = call(
        add_chips,
        [shape((piece, hidden), BF), shape((1, hidden), F32)],
        [VMEM] * (1 + chips),
        own,
        bias_part,
        *received,
    )
    parts = [part] + [over_src(part, m) for m in range(1, n_src)]
    chunk = call(add_bands, shape((piece, hidden), BF), [VMEM] * n_src, *parts)
    near = [chunk] + [over_chips(chunk, m) for m in range(1, chips)]
    far = [over_core(x) for x in near]
    chunks = {(0, m): x for m, x in enumerate(near)} | {(1, m): x for m, x in enumerate(far)}
    last = [(0, chips - 1), (1, chips - 1)]
    first = [w for w in chunks if w not in last]
    weight_grad = None
    for which in (first, last):
        before = [] if weight_grad is None else [weight_grad]
        weight_grad = call(
            functools.partial(spread, which),
            shape((total_rows, hidden), F32),
            [SMEM] + [VMEM] * len(which) + [ANY] * len(before),
            place,
            *[chunks[w] for w in which],
            *before,
            scratch=[
                pltpu.VMEM((len(which), piece, hidden), F32),
                pltpu.SemaphoreType.DMA((len(which),)),
            ],
            aliases={1 + len(which): 0} if before else None,
            out_spec=ANY,
        )
    weight_grad = weight_grad.reshape(relations, width, hidden).transpose(1, 0, 2)
    return output, weight_grad, bias_grad.reshape(hidden)


def solution(mesh):
    in_specs = (
        P(("src", "dst"), None),
        P(),
        P(),
        P("dst", "src", None, None, None, None),
        P("dst", "src", None, None),
        P("dst", "src", None),
        P(("dst", "src"), None),
    )
    out_specs = (P(("dst", "src"), None), P(), P())
    return jax.shard_map(
        on_device, mesh=mesh, in_specs=in_specs, out_specs=out_specs, check_vma=False
    )
```

```python
import functools

import jax
import jax.numpy as jnp
from jax import lax
from jax.experimental import pallas as pl
from jax.experimental.pallas import tpu as pltpu
from jax.sharding import PartitionSpec as P

BF = jnp.bfloat16
F32 = jnp.float32
TAIL = 16
ANY = pl.BlockSpec(memory_space=pl.ANY)
SMEM = pl.BlockSpec(memory_space=pltpu.SMEM)
VMEM = pl.BlockSpec(memory_space=pltpu.VMEM)


def shape(dims, dtype):
    return jax.ShapeDtypeStruct(dims, dtype)


def call(body, out, specs, *args, scratch=(), flops=0, moved=0, out_specs=None):
    return pl.pallas_call(
        body,
        out_shape=out,
        in_specs=list(specs),
        out_specs=out_specs or jax.tree.map(lambda _: VMEM, out),
        scratch_shapes=list(scratch),
        compiler_params=pltpu.CompilerParams(vmem_limit_bytes=24 * 2**20),
        cost_estimate=pl.CostEstimate(flops=flops, bytes_accessed=moved, transcendentals=0),
    )(*args)


def assemble(band_rows, list_ref, count_ref, values_ref, dense_ref, zero_ref):
    zero_ref[...] = jnp.zeros_like(zero_ref)
    slots = values_ref.shape[0] // count_ref.shape[0]
    size = values_ref.shape[1]
    across = dense_ref.shape[1] // size
    dense_ref[...] = jnp.zeros_like(dense_ref)

    def place(at, carry):
        relation = lax.div(at, slots)

        @pl.when(lax.rem(at, slots) < count_ref[relation])
        def _():
            k = list_ref[relation, lax.rem(at, slots)]
            row = pl.multiple_of(relation * band_rows + lax.div(k, across) * size, size)
            column = pl.multiple_of(lax.rem(k, across) * size, size)
            dense_ref[pl.ds(row, size), pl.ds(column, size)] = values_ref[at]

        return carry

    lax.fori_loop(0, values_ref.shape[0], place, 0)


def collect(here, pieces, features):
    rows = pieces[0].shape[0]
    for k, piece in enumerate(pieces):
        features[pl.ds(pl.multiple_of((here ^ k) * rows, 16), rows)] = piece[...]


def forward_near(count, dense_ref, *refs):
    pieces, (total_ref, features) = refs[:count], refs[count:]
    me = lax.axis_index("dst")
    collect(lax.rem(me, count), pieces, features)
    depth = features.shape[0]
    columns = pl.ds(pl.multiple_of(lax.div(me, count) * depth, 128), depth)
    step = 384
    for i in range(0, total_ref.shape[0], step):
        total_ref[i : i + step] = jnp.dot(
            dense_ref[i : i + step, columns], features[...], preferred_element_type=F32
        )


def forward(count, dense_ref, weight_ref, total_ref, *refs):
    pieces, (tile_ref, own_ref, *sends, features, message) = refs[:count], refs[count:]
    me = lax.axis_index("dst")
    collect(lax.rem(me, count), pieces, features)
    depth, width = features.shape
    columns = pl.ds(pl.multiple_of((1 - lax.div(me, count)) * depth, 128), depth)
    band_rows = tile_ref.shape[0]
    step = 128
    for i in range(0, band_rows, step):
        for r in range(dense_ref.shape[0] // band_rows):
            at = slice(r * band_rows + i, r * band_rows + i + step)
            part = jnp.dot(
                dense_ref[at, columns], features[...], preferred_element_type=F32
            )
            tile_ref[i : i + step, r * width : (r + 1) * width] = (total_ref[at] + part).astype(BF)
    message[...] = jnp.dot(tile_ref[...], weight_ref[...], preferred_element_type=F32)
    block = own_ref.shape[0]
    z = lax.axis_index("src")
    for m in range(len(sends) + 1):
        mine = message[pl.ds(pl.multiple_of((z ^ m) * block, 16), block)]
        if m == 0:
            own_ref[...] = mine
        else:
            sends[m - 1][...] = mine.astype(BF)


def transpose(tile_ref, pre_ref, out_ref, output_ref):
    pre = pre_ref[...]
    output_ref[...] = (pre * jax.nn.sigmoid(pre)).astype(BF)
    step = 256
    for at in range(0, tile_ref.shape[1], step):
        out_ref[at : at + step] = tile_ref[:, at : at + step].T


def activate(bias_ref, cotangent_ref, own_ref, *refs):
    *others, pre_ref, grad_ref = refs
    pre = own_ref[...]
    for other in others:
        pre = pre + other[...].astype(F32)
    pre = pre + bias_ref[...].astype(F32)
    sigma = jax.nn.sigmoid(pre)
    pre_ref[...] = pre
    grad_ref[...] = (
        cotangent_ref[...].astype(F32) * sigma * (1.0 + pre * (1.0 - sigma))
    ).astype(BF)


def split_row(row):
    at = lax.broadcasted_iota(jnp.int32, (TAIL, row.shape[1]), 0)
    high = row.astype(BF).astype(F32)
    return jnp.where(at == 0, high, jnp.where(at == 1, row - high, 0.0)).astype(BF)


def join_row(tail):
    return jnp.sum(tail.astype(F32), axis=0, keepdims=True)


def backward(chips, tile_ref, *refs):
    *grads, keep_ref, send_ref, bias_ref, grad = refs
    z, me = lax.axis_index("src"), lax.axis_index("dst")
    block = grads[0].shape[0]
    for m, piece in enumerate(grads):
        grad[pl.ds(pl.multiple_of((z ^ m) * block, 16), block)] = piece[...]
    piece = keep_ref.shape[0] // chips
    half = tile_ref.shape[0] // 2
    bias = jnp.sum(grad[...].astype(F32), axis=0, keepdims=True)
    tail = split_row(bias)
    bias_ref[...] = jnp.broadcast_to(join_row(tail), bias_ref.shape)
    send_ref[pl.ds(piece * chips, TAIL)] = tail
    for ref, core in ((send_ref, 1 - lax.rem(me, 2)), (keep_ref, lax.rem(me, 2))):
        for m in range(chips):
            start = pl.multiple_of(core * half + (lax.div(me, 2) ^ m) * piece, 16)
            ref[m * piece : (m + 1) * piece] = jnp.dot(
                tile_ref[pl.ds(start, piece)], grad[...], preferred_element_type=F32
            ).astype(ref.dtype)


def add_cores(chips, keep_ref, bias_ref, received_ref, own_ref, total_ref, *sends):
    piece = own_ref.shape[0]
    tail = split_row(bias_ref[0:1] + join_row(received_ref[pl.ds(piece * chips, TAIL)]))
    total_ref[...] = jnp.broadcast_to(join_row(tail), total_ref.shape)
    for m in range(chips):
        at = pl.ds(m * piece, piece)
        both = keep_ref[at] + received_ref[at].astype(F32)
        if m == 0:
            own_ref[...] = both
        else:
            sends[m - 1][0:piece] = both.astype(BF)
            sends[m - 1][piece : piece + TAIL] = tail


def tree(terms):
    while len(terms) > 1:
        terms = [a + b for a, b in zip(terms[::2], terms[1::2])]
    return terms[0]


def add_chips(own_ref, bias_ref, *refs):
    *received, sum_ref, total_ref = refs
    piece = own_ref.shape[0]
    tails = [join_row(other[pl.ds(piece, TAIL)]) for other in received]
    total_ref[...] = jnp.broadcast_to(tree([bias_ref[0:1]] + tails), total_ref.shape)
    parts = [other[0:piece].astype(F32) for other in received]
    sum_ref[...] = tree([own_ref[...]] + parts).astype(BF)


def add_bands(*refs):
    *parts, out_ref = refs
    out_ref[...] = tree([part[...].astype(F32) for part in parts]).astype(BF)


def spread(bias_ref, *refs):
    me = lax.axis_index("dst")
    *chunks, out_ref, row_ref, wide, sems = refs
    row_ref[...] = bias_ref[0:1]
    rows = chunks[0].shape[0]
    half = out_ref.shape[0] // 2
    chips = len(chunks) // 2
    copies = []
    for i, chunk in enumerate(chunks):
        wide[i] = chunk[...].astype(F32)
        start = (lax.rem(me, 2) ^ (i // chips)) * half + (lax.div(me, 2) ^ (i % chips)) * rows
        target = out_ref.at[pl.ds(pl.multiple_of(start, 16), rows)]
        copies.append(pltpu.make_async_copy(wide.at[i], target, sems.at[i]))
        copies[-1].start()
    for copy in copies:
        copy.wait()


def swap(x, axis, n, mask):
    return lax.ppermute(x, axis, [(i, i ^ mask) for i in range(n)])


def on_device(features, relation_weight, bias, block_values, block_list, block_count, cotangent):
    n_dst, n_src = lax.axis_size("dst"), lax.axis_size("src")
    own_rows, width = features.shape
    relations, hidden = relation_weight.shape[1:]
    block_size = block_values.shape[5]
    tile_columns = own_rows * n_dst
    block = cotangent.shape[0]
    band_rows = block * n_src
    few = n_dst == 8 and n_src == 4 and (relations * width) % (8 * 16) == 0
    weight = relation_weight.transpose(1, 0, 2).reshape(relations * width, hidden)
    dense, zero = call(
        functools.partial(assemble, band_rows),
        [shape((relations * band_rows, tile_columns), BF), shape(features.shape, BF)],
        (SMEM, SMEM, VMEM),
        block_list.reshape(relations, -1),
        block_count.reshape(-1),
        block_values.reshape(-1, block_size, block_size),
        flops=10**8,
        moved=4 * 2**20,
    )
    if few:
        return few_devices(features, weight, bias, dense, zero, cotangent, relations)
    gathered = lax.all_gather(features, "dst", axis=0, tiled=True)
    tile = jnp.dot(dense, gathered, preferred_element_type=F32).astype(BF)
    tile = tile.reshape(relations, band_rows, width)
    partial = jnp.einsum(
        "rnd,rdh->nh",
        tile,
        weight.reshape(relations, width, hidden),
        preferred_element_type=F32,
    )
    pre = lax.psum_scatter(partial, "src", scatter_dimension=0, tiled=True)
    pre = pre + bias.astype(F32)
    sigma = jax.nn.sigmoid(pre)
    output = (pre * sigma).astype(BF)
    grad = (cotangent.astype(F32) * sigma * (1.0 + pre * (1.0 - sigma))).astype(BF)
    band_grad = lax.all_gather(grad, "src", axis=0, tiled=True)
    weight_term = jnp.einsum("rnd,nh->rdh", tile, band_grad, preferred_element_type=F32)
    weight_grad, bias_grad = lax.psum(
        (weight_term, jnp.sum(grad.astype(F32), axis=0)), ("dst", "src")
    )
    return output, weight_grad.transpose(1, 0, 2), bias_grad


def few_devices(features, weight, bias, dense, zero, cotangent, relations):
    n_dst, n_src = lax.axis_size("dst"), lax.axis_size("src")
    chips = n_dst // 2
    own_rows, width = features.shape
    block, hidden = cotangent.shape
    band_rows = block * n_src
    total_rows = weight.shape[0]
    piece = total_rows // n_dst
    half = n_dst // 2

    def over_chips(x, m):
        return swap(x, "dst", n_dst, 2 * m)

    def over_core(x):
        return swap(x, "dst", n_dst, 1)

    def over_src(x, m):
        return swap(x, "src", n_src, m)

    near = [features] + [over_chips(features, m) for m in range(1, chips)]
    near[1] = near[1] + zero
    far = [over_core(x) for x in near]
    pieces = [x for pair in zip(near, far) for x in pair]
    total = call(
        functools.partial(forward_near, half),
        shape((relations * band_rows, width), F32),
        [VMEM] * (1 + half),
        dense,
        *pieces[:half],
        scratch=[pltpu.VMEM((own_rows * half, width), BF)],
        flops=10**9,
        moved=2**20,
    )
    tile, own, *sends = call(
        functools.partial(forward, half),
        [shape((band_rows, relations * width), BF), shape((block, hidden), F32)]
        + [shape((block, hidden), BF)] * (n_src - 1),
        [VMEM] * (3 + half),
        dense,
        weight,
        total,
        *pieces[half:],
        scratch=[
            pltpu.VMEM((own_rows * half, width), BF),
            pltpu.VMEM((band_rows, hidden), F32),
        ],
        flops=10**9,
        moved=2**20,
    )
    received = [over_src(x, m + 1) for m, x in enumerate(sends)]
    pre, grad = call(
        activate,
        [shape((block, hidden), F32), shape((block, hidden), BF)],
        [VMEM] * (2 + n_src),
        bias.reshape(1, hidden),
        cotangent,
        own,
        *received,
    )
    turned, output = call(
        transpose,
        [shape((total_rows, band_rows), BF), shape((block, hidden), BF)],
        [VMEM] * 2,
        tile,
        pre,
        flops=10**8,
        moved=4 * 2**20,
    )
    keep, send, bias_part = call(
        functools.partial(backward, chips),
        [
            shape((piece * chips, hidden), F32),
            shape((piece * chips + TAIL, hidden), BF),
            shape((8, hidden), F32),
        ],
        [VMEM] * (1 + n_src),
        turned,
        grad,
        *[over_src(grad, m) for m in range(1, n_src)],
        scratch=[pltpu.VMEM((band_rows, hidden), BF)],
    )
    own, bias_part, *sends = call(
        functools.partial(add_cores, chips),
        [shape((piece, hidden), F32), shape((8, hidden), F32)]
        + [shape((piece + TAIL, hidden), BF)] * (chips - 1),
        [VMEM] * 3,
        keep,
        bias_part,
        over_core(send),
    )
    received = [over_chips(x, m + 1) for m, x in enumerate(sends)]
    part, bias_grad = call(
        add_chips,
        [shape((piece, hidden), BF), shape((8, hidden), F32)],
        [VMEM] * (1 + chips),
        own,
        bias_part,
        *received,
    )
    parts = [part] + [over_src(part, m) for m in range(1, n_src)]
    chunk = call(add_bands, shape((piece, hidden), BF), [VMEM] * n_src, *parts)
    near = [chunk] + [over_chips(chunk, m) for m in range(1, chips)]
    far = [over_core(x) for x in near]
    weight_grad, bias_grad = call(
        spread,
        [shape((total_rows, hidden), F32), shape((1, hidden), F32)],
        [VMEM] * (1 + n_dst),
        bias_grad,
        *near,
        *far,
        scratch=[pltpu.VMEM((n_dst, piece, hidden), F32), pltpu.SemaphoreType.DMA((n_dst,))],
        out_specs=[ANY, VMEM],
    )
    weight_grad = weight_grad.reshape(relations, width, hidden).transpose(1, 0, 2)
    return output, weight_grad, bias_grad.reshape(hidden)


def solution(mesh):
    in_specs = (
        P(("src", "dst"), None),
        P(),
        P(),
        P("dst", "src", None, None, None, None),
        P("dst", "src", None, None),
        P("dst", "src", None),
        P(("dst", "src"), None),
    )
    out_specs = (P(("dst", "src"), None), P(), P())
    return jax.shard_map(
        on_device, mesh=mesh, in_specs=in_specs, out_specs=out_specs, check_vma=False
    )
```

```python
import functools

import jax
import jax.numpy as jnp
from jax import lax
from jax.experimental import pallas as pl
from jax.experimental.pallas import tpu as pltpu
from jax.sharding import PartitionSpec as P

BF = jnp.bfloat16
F32 = jnp.float32
MESSAGE = (3, 2, 1)
GRAD = (1, 2, 3)
SUMS = (1, 2, 3)
CHUNKS = (1, 2, 3)
FIRST, REST = (1, 2), (3, 0)
FAR = (3, 2)
TAIL = 16
ANY = pl.BlockSpec(memory_space=pl.ANY)
SMEM = pl.BlockSpec(memory_space=pltpu.SMEM)
VMEM = pl.BlockSpec(memory_space=pltpu.VMEM)


def shape(dims, dtype):
    return jax.ShapeDtypeStruct(dims, dtype)


def call(body, out, specs, *args, scratch=(), flops=0, moved=0, out_specs=None, aliases=None):
    return pl.pallas_call(
        body,
        out_shape=out,
        in_specs=list(specs),
        out_specs=out_specs or jax.tree.map(lambda _: VMEM, out),
        scratch_shapes=list(scratch),
        input_output_aliases=aliases or {},
        compiler_params=pltpu.CompilerParams(vmem_limit_bytes=24 * 2**20),
        cost_estimate=pl.CostEstimate(flops=flops, bytes_accessed=moved, transcendentals=0),
    )(*args)


def assemble(band_rows, list_ref, count_ref, values_ref, dense_ref, zero_ref):
    zero_ref[...] = jnp.zeros_like(zero_ref)
    slots = values_ref.shape[0] // count_ref.shape[0]
    size = values_ref.shape[1]
    across = dense_ref.shape[1] // size
    dense_ref[...] = jnp.zeros_like(dense_ref)

    def place(at, carry):
        relation = lax.div(at, slots)

        @pl.when(lax.rem(at, slots) < count_ref[relation])
        def _():
            k = list_ref[relation, lax.rem(at, slots)]
            row = pl.multiple_of(relation * band_rows + lax.div(k, across) * size, size)
            column = pl.multiple_of(lax.rem(k, across) * size, size)
            dense_ref[pl.ds(row, size), pl.ds(column, size)] = values_ref[at]

        return carry

    lax.fori_loop(0, values_ref.shape[0], place, 0)


def collect(here, pieces, features):
    rows = pieces[0].shape[0]
    for k, piece in enumerate(pieces):
        features[pl.ds(pl.multiple_of((here ^ k) * rows, 16), rows)] = piece[...]


def half_message(dense_ref, weight_ref, features, half):
    depth, width = features.shape
    columns = pl.ds(pl.multiple_of(half * depth, 128), depth)
    relations = weight_ref.shape[0] // width
    rows = dense_ref.shape[0] // relations
    total = None
    for r in range(relations):
        projected = jnp.dot(
            features[...],
            weight_ref[r * width : (r + 1) * width],
            preferred_element_type=F32,
        ).astype(BF)
        term = jnp.dot(
            dense_ref[r * rows : (r + 1) * rows, columns],
            projected,
            preferred_element_type=F32,
        )
        total = term if total is None else total + term
    return total


def forward_near(dense_ref, weight_ref, *refs):
    *pieces, message_ref, features_ref = refs
    me, count = lax.axis_index("dst"), len(pieces)
    collect(lax.rem(me, count), pieces, features_ref)
    message_ref[...] = half_message(dense_ref, weight_ref, features_ref, lax.div(me, count))


def forward(count, dense_ref, weight_ref, near_ref, *refs):
    pieces, (features_ref, own_ref, *sends, message) = refs[:count], refs[count:]
    me, z = lax.axis_index("dst"), lax.axis_index("src")
    collect(lax.rem(me, count) ^ (2 * (FAR[0] - 2)), pieces, features_ref)
    message[...] = near_ref[...] + half_message(
        dense_ref, weight_ref, features_ref, 1 - lax.div(me, count)
    )
    block = own_ref.shape[0]
    for m in range(len(sends) + 1):
        mine = message[pl.ds(pl.multiple_of((z ^ m) * block, 16), block)]
        if m == 0:
            own_ref[...] = mine
        else:
            sends[m - 1][...] = mine.astype(BF)


def tile_turned(count, dense_ref, near_ref, far_ref, out_ref, features):
    half = lax.div(lax.axis_index("dst"), count)
    depth, width = near_ref.shape
    features[pl.ds(pl.multiple_of(half * depth, 128), depth)] = near_ref[...]
    features[pl.ds(pl.multiple_of((1 - half) * depth, 128), depth)] = far_ref[...]
    rows = out_ref.shape[1]
    step = 256
    for r in range(dense_ref.shape[0] // rows):
        for at in range(0, width, step):
            part = jnp.dot(
                dense_ref[r * rows : (r + 1) * rows],
                features[:, at : at + step],
                preferred_element_type=F32,
            )
            out_ref[r * width + at : r * width + at + step] = part.astype(BF).T


def activate(bias_ref, cotangent_ref, own_ref, *refs):
    *others, pre_ref, grad_ref = refs
    pre = own_ref[...]
    for other in others:
        pre = pre + other[...].astype(F32)
    pre = pre + bias_ref[...].astype(F32)
    sigma = jax.nn.sigmoid(pre)
    pre_ref[...] = pre
    grad_ref[...] = (
        cotangent_ref[...].astype(F32) * sigma * (1.0 + pre * (1.0 - sigma))
    ).astype(BF)


def tree(terms):
    while len(terms) > 1:
        terms = [a + b for a, b in zip(terms[::2], terms[1::2])]
    return terms[0]


def split_row(row):
    at = lax.broadcasted_iota(jnp.int32, (TAIL, row.shape[1]), 0)
    high = row.astype(BF).astype(F32)
    return jnp.where(at == 0, high, jnp.where(at == 1, row - high, 0.0)).astype(BF)


def join_row(tail):
    return jnp.sum(tail.astype(F32), axis=0, keepdims=True)


def half_gradient(core, which, chips, tile_ref, grad, out_ref, piece):
    chip = lax.div(lax.axis_index("dst"), 2)
    for i, m in enumerate(which):
        start = pl.multiple_of((core * chips + (chip ^ m)) * piece, 16)
        out_ref[i * piece : (i + 1) * piece] = jnp.dot(
            tile_ref[pl.ds(start, piece)], grad, preferred_element_type=F32
        ).astype(out_ref.dtype)


def backward_first(chips, tile_ref, *refs):
    *grads, send_ref, bias_ref, grad_ref = refs
    block = grads[0].shape[0]
    z = lax.axis_index("src")
    grads = dict(zip((0, *GRAD), grads))
    for m, piece in grads.items():
        grad_ref[pl.ds(pl.multiple_of((z ^ m) * block, 16), block)] = piece[...]
    rows = [
        jnp.sum(grads[m][...].astype(F32), axis=0, keepdims=True) for m in range(len(grads))
    ]
    tail = split_row(tree(rows))
    bias_ref[...] = jnp.broadcast_to(join_row(tail), bias_ref.shape)
    piece = (send_ref.shape[0] - TAIL) // len(FIRST)
    send_ref[pl.ds(piece * len(FIRST), TAIL)] = tail
    other = 1 - lax.rem(lax.axis_index("dst"), 2)
    half_gradient(other, FIRST, chips, tile_ref, grad_ref[...], send_ref, piece)


def backward_rest(chips, tile_ref, grad_ref, send_ref):
    other = 1 - lax.rem(lax.axis_index("dst"), 2)
    piece = send_ref.shape[0] // len(REST)
    half_gradient(other, REST, chips, tile_ref, grad_ref[...], send_ref, piece)


def backward_keep(chips, tile_ref, grad_ref, keep_ref):
    core = lax.rem(lax.axis_index("dst"), 2)
    piece = keep_ref.shape[0] // chips
    half_gradient(core, range(chips), chips, tile_ref, grad_ref[...], keep_ref, piece)


def add_first(keep_ref, bias_ref, received_ref, total_ref, *sends):
    piece = sends[0].shape[0] - TAIL
    tail = split_row(bias_ref[0:1] + join_row(received_ref[pl.ds(piece * len(FIRST), TAIL)]))
    total_ref[...] = jnp.broadcast_to(join_row(tail), total_ref.shape)
    for i, m in enumerate(FIRST):
        both = keep_ref[pl.ds(m * piece, piece)]
        both = both + received_ref[pl.ds(i * piece, piece)].astype(F32)
        sends[i][0:piece] = both.astype(BF)
        sends[i][piece : piece + TAIL] = tail


def add_rest(keep_ref, total_ref, received_ref, own_ref, *sends):
    piece = own_ref.shape[0]
    for i, m in enumerate(REST):
        both = keep_ref[pl.ds(m * piece, piece)]
        both = both + received_ref[pl.ds(i * piece, piece)].astype(F32)
        if m == 0:
            own_ref[...] = both
        else:
            sends[i][0:piece] = both.astype(BF)
            sends[i][piece : piece + TAIL] = split_row(total_ref[0:1])


def add_chips(own_ref, bias_ref, *refs):
    *received, sum_ref, total_ref = refs
    received = [received[SUMS.index(m)] for m in range(1, len(received) + 1)]
    piece = own_ref.shape[0]
    tails = [join_row(other[pl.ds(piece, TAIL)]) for other in received]
    total_ref[...] = jnp.broadcast_to(tree([bias_ref[0:1]] + tails), total_ref.shape)
    parts = [other[0:piece].astype(F32) for other in received]
    sum_ref[...] = tree([own_ref[...]] + parts).astype(BF)


def add_bands(*refs):
    *parts, out_ref = refs
    out_ref[...] = tree([part[...].astype(F32) for part in parts]).astype(BF)


def spread(which, chunks, out_ref, wide, sems, copies=()):
    me = lax.axis_index("dst")
    rows = chunks[0].shape[0]
    copies = list(copies)
    half = out_ref.shape[0] // 2
    for i, (core, chip) in enumerate(which):
        wide[i] = chunks[i][...].astype(F32)
        start = (lax.rem(me, 2) ^ core) * half + (lax.div(me, 2) ^ chip) * rows
        target = out_ref.at[pl.ds(pl.multiple_of(start, 16), rows)]
        copies.append(pltpu.make_async_copy(wide.at[i], target, sems.at[i]))
        copies[-1].start()
    for copy in copies:
        copy.wait()


def spread_first(which, bias_ref, pre_ref, *refs):
    *chunks, out_ref, row_ref, output_ref, wide, active, sems = refs
    pre = pre_ref[...]
    active[...] = (pre * jax.nn.sigmoid(pre)).astype(BF)
    copies = [
        pltpu.make_async_copy(bias_ref.at[pl.ds(0, 1)], row_ref, sems.at[len(which)]),
        pltpu.make_async_copy(active, output_ref, sems.at[len(which) + 1]),
    ]
    for copy in copies:
        copy.start()
    spread(which, chunks, out_ref, wide, sems, copies)


def spread_last(which, *refs):
    *chunks, _, out_ref, wide, sems = refs
    spread(which, chunks, out_ref, wide, sems)


def swap(x, axis, n, mask):
    return lax.ppermute(x, axis, [(i, i ^ mask) for i in range(n)])


def on_device(features, relation_weight, bias, block_values, block_list, block_count, cotangent):
    n_dst, n_src = lax.axis_size("dst"), lax.axis_size("src")
    own_rows, width = features.shape
    relations, hidden = relation_weight.shape[1:]
    block_size = block_values.shape[5]
    tile_columns = own_rows * n_dst
    block = cotangent.shape[0]
    band_rows = block * n_src
    few = n_dst == 8 and n_src == 4 and (relations * width) % (8 * 16) == 0
    weight = relation_weight.transpose(1, 0, 2).reshape(relations * width, hidden)
    dense, zero = call(
        functools.partial(assemble, band_rows),
        [shape((relations * band_rows, tile_columns), BF), shape(features.shape, BF)],
        (SMEM, SMEM, VMEM),
        block_list.reshape(relations, -1),
        block_count.reshape(-1),
        block_values.reshape(-1, block_size, block_size),
        flops=10**8,
        moved=4 * 2**20,
    )
    if few:
        return few_devices(features, weight, bias, dense, zero, cotangent, relations)
    gathered = lax.all_gather(features, "dst", axis=0, tiled=True)
    tile = jnp.dot(dense, gathered, preferred_element_type=F32).astype(BF)
    tile = tile.reshape(relations, band_rows, width)
    partial = jnp.einsum(
        "rnd,rdh->nh",
        tile,
        weight.reshape(relations, width, hidden),
        preferred_element_type=F32,
    )
    pre = lax.psum_scatter(partial, "src", scatter_dimension=0, tiled=True)
    pre = pre + bias.astype(F32)
    sigma = jax.nn.sigmoid(pre)
    output = (pre * sigma).astype(BF)
    grad = (cotangent.astype(F32) * sigma * (1.0 + pre * (1.0 - sigma))).astype(BF)
    band_grad = lax.all_gather(grad, "src", axis=0, tiled=True)
    weight_term = jnp.einsum("rnd,nh->rdh", tile, band_grad, preferred_element_type=F32)
    weight_grad, bias_grad = lax.psum(
        (weight_term, jnp.sum(grad.astype(F32), axis=0)), ("dst", "src")
    )
    return output, weight_grad.transpose(1, 0, 2), bias_grad


def few_devices(features, weight, bias, dense, zero, cotangent, relations):
    n_dst, n_src = lax.axis_size("dst"), lax.axis_size("src")
    chips = n_dst // 2
    own_rows, width = features.shape
    block, hidden = cotangent.shape
    band_rows = block * n_src
    total_rows = weight.shape[0]
    piece = total_rows // n_dst
    half = n_dst // 2

    def over_chips(x, m):
        return swap(x, "dst", n_dst, 2 * m)

    def over_core(x):
        return swap(x, "dst", n_dst, 1)

    def over_src(x, m):
        return swap(x, "src", n_src, m)

    near = [features] + [over_chips(features, m) for m in range(1, chips)]
    near[1] = near[1] + zero
    far = [over_core(x) for x in near]
    pieces = [x for pair in zip(near, far) for x in pair]
    half = n_dst // 2
    half_shape = shape((own_rows * half, width), BF)
    message_near, features_near = call(
        forward_near,
        [shape((band_rows, hidden), F32), half_shape],
        [VMEM] * (2 + half),
        dense,
        weight,
        *pieces[:half],
        flops=10**9,
        moved=2**20,
    )
    features_far, own, *sends = call(
        functools.partial(forward, half),
        [half_shape, shape((block, hidden), F32)] + [shape((block, hidden), BF)] * (n_src - 1),
        [VMEM] * (3 + half),
        dense,
        weight,
        message_near,
        *[x for m in FAR for x in (near[m], far[m])],
        scratch=[pltpu.VMEM((band_rows, hidden), F32)],
        flops=10**9,
        moved=2**20,
    )
    received = [over_src(x, m + 1) for m, x in enumerate(sends)]
    turned = call(
        functools.partial(tile_turned, half),
        shape((total_rows, band_rows), BF),
        [VMEM] * 3,
        dense,
        features_near,
        features_far,
        scratch=[pltpu.VMEM((own_rows * n_dst, width), BF)],
        flops=2 * 10**9,
        moved=4 * 2**20,
    )
    pre, grad = call(
        activate,
        [shape((block, hidden), F32), shape((block, hidden), BF)],
        [VMEM] * (2 + n_src),
        bias.reshape(1, hidden),
        cotangent,
        own,
        *[received[m - 1] for m in MESSAGE],
    )
    first, bias_part, band_grad = call(
        functools.partial(backward_first, chips),
        [
            shape((piece * len(FIRST) + TAIL, hidden), BF),
            shape((8, hidden), F32),
            shape((band_rows, hidden), BF),
        ],
        [VMEM] * (1 + n_src),
        turned,
        grad,
        *[over_src(grad, m) for m in GRAD],
    )
    rest = call(
        functools.partial(backward_rest, chips),
        shape((piece * len(REST), hidden), BF),
        [VMEM] * 2,
        turned,
        band_grad,
        flops=3 * 10**8,
        moved=2**20,
    )
    keep = call(
        functools.partial(backward_keep, chips),
        shape((piece * chips, hidden), F32),
        [VMEM] * 2,
        turned,
        band_grad,
        flops=3 * 10**8,
        moved=2**20,
    )
    sent = shape((piece + TAIL, hidden), BF)
    bias_part, *sends = call(
        add_first,
        [shape((8, hidden), F32)] + [sent] * len(FIRST),
        [VMEM] * 3,
        keep,
        bias_part,
        over_core(first),
    )
    own, *others = call(
        add_rest,
        [shape((piece, hidden), F32)] + [sent] * (len(REST) - 1),
        [VMEM] * 3,
        keep,
        bias_part,
        over_core(rest),
    )
    sends = dict(zip(FIRST, sends)) | dict(zip(REST, others))
    received = {m: over_chips(x, m) for m, x in sends.items()}
    part, bias_sum = call(
        add_chips,
        [shape((piece, hidden), BF), shape((8, hidden), F32)],
        [VMEM] * (1 + chips),
        own,
        bias_part,
        *[received[m] for m in SUMS],
    )
    chunk = part
    for m in (1, 3):
        chunk = call(
            add_bands, shape((piece, hidden), BF), [VMEM] * 2, chunk, over_src(chunk, m)
        )
    near = [chunk] + [over_chips(chunk, m) for m in range(1, chips)]
    far = [over_core(x) for x in near]
    chunks = {(0, m): x for m, x in enumerate(near)} | {(1, m): x for m, x in enumerate(far)}
    last = [(0, CHUNKS[-1]), (1, CHUNKS[-1])]
    first = [(core, m) for core in range(2) for m in (0, *CHUNKS[:-1])]
    whole = shape((total_rows, hidden), F32)

    weight_grad, bias_grad, output = call(
        functools.partial(spread_first, first),
        [whole, shape((1, hidden), F32), shape((block, hidden), BF)],
        [VMEM] * (2 + len(first)),
        bias_sum,
        pre,
        *[chunks[w] for w in first],
        scratch=[
            pltpu.VMEM((len(first), piece, hidden), F32),
            pltpu.VMEM((block, hidden), BF),
            pltpu.SemaphoreType.DMA((len(first) + 2,)),
        ],
        out_specs=[ANY] * 3,
    )
    weight_grad = call(
        functools.partial(spread_last, last),
        whole,
        [VMEM] * len(last) + [ANY],
        *[chunks[w] for w in last],
        weight_grad,
        scratch=[
            pltpu.VMEM((len(last), piece, hidden), F32),
            pltpu.SemaphoreType.DMA((len(last),)),
        ],
        aliases={len(last): 0},
        out_specs=ANY,
    )
    weight_grad = weight_grad.reshape(relations, width, hidden).transpose(1, 0, 2)
    return output, weight_grad, bias_grad.reshape(hidden)


def solution(mesh):
    in_specs = (
        P(("src", "dst"), None),
        P(),
        P(),
        P("dst", "src", None, None, None, None),
        P("dst", "src", None, None),
        P("dst", "src", None),
        P(("dst", "src"), None),
    )
    out_specs = (P(("dst", "src"), None), P(), P())
    return jax.shard_map(
        on_device, mesh=mesh, in_specs=in_specs, out_specs=out_specs, check_vma=False
    )
```

```python
import functools

import jax
import jax.numpy as jnp
from jax import lax
from jax.experimental import pallas as pl
from jax.experimental.pallas import tpu as pltpu
from jax.sharding import PartitionSpec as P

BF = jnp.bfloat16
F32 = jnp.float32
MESSAGE = (2, 3, 1)
GRAD = (1, 2, 3)
SUMS = (1, 2, 3)
CHUNKS = (1, 2, 3)
FIRST, REST = (2, 1), (3, 0)
FAR = (3, 2)
TAIL = 16
ANY = pl.BlockSpec(memory_space=pl.ANY)
SMEM = pl.BlockSpec(memory_space=pltpu.SMEM)
VMEM = pl.BlockSpec(memory_space=pltpu.VMEM)


def shape(dims, dtype):
    return jax.ShapeDtypeStruct(dims, dtype)


def call(body, out, specs, *args, scratch=(), flops=0, moved=0, out_specs=None, aliases=None):
    return pl.pallas_call(
        body,
        out_shape=out,
        in_specs=list(specs),
        out_specs=out_specs or jax.tree.map(lambda _: VMEM, out),
        scratch_shapes=list(scratch),
        input_output_aliases=aliases or {},
        compiler_params=pltpu.CompilerParams(vmem_limit_bytes=24 * 2**20),
        cost_estimate=pl.CostEstimate(flops=flops, bytes_accessed=moved, transcendentals=0),
    )(*args)


def assemble(band_rows, list_ref, count_ref, values_ref, dense_ref, zero_ref):
    zero_ref[...] = jnp.zeros_like(zero_ref)
    slots = values_ref.shape[0] // count_ref.shape[0]
    size = values_ref.shape[1]
    across = dense_ref.shape[1] // size
    dense_ref[...] = jnp.zeros_like(dense_ref)

    def place(at, carry):
        relation = lax.div(at, slots)

        @pl.when(lax.rem(at, slots) < count_ref[relation])
        def _():
            k = list_ref[relation, lax.rem(at, slots)]
            row = pl.multiple_of(relation * band_rows + lax.div(k, across) * size, size)
            column = pl.multiple_of(lax.rem(k, across) * size, size)
            dense_ref[pl.ds(row, size), pl.ds(column, size)] = values_ref[at]

        return carry

    lax.fori_loop(0, values_ref.shape[0], place, 0)


def collect(here, pieces, features):
    rows = pieces[0].shape[0]
    for k, piece in enumerate(pieces):
        features[pl.ds(pl.multiple_of((here ^ k) * rows, 16), rows)] = piece[...]


def half_message(dense_ref, weight_ref, features, half):
    depth, width = features.shape
    columns = pl.ds(pl.multiple_of(half * depth, 128), depth)
    relations = weight_ref.shape[0] // width
    rows = dense_ref.shape[0] // relations
    total = None
    for r in range(relations):
        projected = jnp.dot(
            features[...],
            weight_ref[r * width : (r + 1) * width],
            preferred_element_type=F32,
        ).astype(BF)
        term = jnp.dot(
            dense_ref[r * rows : (r + 1) * rows, columns],
            projected,
            preferred_element_type=F32,
        )
        total = term if total is None else total + term
    return total


def forward_near(dense_ref, weight_ref, *refs):
    *pieces, message_ref, features_ref = refs
    me, count = lax.axis_index("dst"), len(pieces)
    collect(lax.rem(me, count), pieces, features_ref)
    message_ref[...] = half_message(dense_ref, weight_ref, features_ref, lax.div(me, count))


def forward(count, dense_ref, weight_ref, near_ref, *refs):
    pieces, (features_ref, own_ref, *sends, message) = refs[:count], refs[count:]
    me, z = lax.axis_index("dst"), lax.axis_index("src")
    collect(lax.rem(me, count) ^ (2 * (FAR[0] - 2)), pieces, features_ref)
    message[...] = near_ref[...] + half_message(
        dense_ref, weight_ref, features_ref, 1 - lax.div(me, count)
    )
    block = own_ref.shape[0]
    for m in range(len(sends) + 1):
        mine = message[pl.ds(pl.multiple_of((z ^ m) * block, 16), block)]
        if m == 0:
            own_ref[...] = mine
        else:
            sends[m - 1][...] = mine.astype(BF)


def tile_turned(count, dense_ref, near_ref, far_ref, out_ref, features):
    half = lax.div(lax.axis_index("dst"), count)
    depth, width = near_ref.shape
    features[pl.ds(pl.multiple_of(half * depth, 128), depth)] = near_ref[...]
    features[pl.ds(pl.multiple_of((1 - half) * depth, 128), depth)] = far_ref[...]
    rows = out_ref.shape[1]
    step = 256
    for r in range(dense_ref.shape[0] // rows):
        for at in range(0, width, step):
            part = jnp.dot(
                dense_ref[r * rows : (r + 1) * rows],
                features[:, at : at + step],
                preferred_element_type=F32,
            )
            out_ref[r * width + at : r * width + at + step] = part.astype(BF).T


def activate(bias_ref, cotangent_ref, own_ref, *refs):
    *others, pre_ref, grad_ref = refs
    pre = own_ref[...]
    for other in others:
        pre = pre + other[...].astype(F32)
    pre = pre + bias_ref[...].astype(F32)
    sigma = jax.nn.sigmoid(pre)
    pre_ref[...] = pre
    grad_ref[...] = (
        cotangent_ref[...].astype(F32) * sigma * (1.0 + pre * (1.0 - sigma))
    ).astype(BF)


def tree(terms):
    while len(terms) > 1:
        terms = [a + b for a, b in zip(terms[::2], terms[1::2])]
    return terms[0]


def split_row(row):
    at = lax.broadcasted_iota(jnp.int32, (TAIL, row.shape[1]), 0)
    high = row.astype(BF).astype(F32)
    return jnp.where(at == 0, high, jnp.where(at == 1, row - high, 0.0)).astype(BF)


def join_row(tail):
    return jnp.sum(tail.astype(F32), axis=0, keepdims=True)


def half_gradient(core, which, chips, tile_ref, grad, out_ref, piece):
    chip = lax.div(lax.axis_index("dst"), 2)
    for i, m in enumerate(which):
        start = pl.multiple_of((core * chips + (chip ^ m)) * piece, 16)
        out_ref[i * piece : (i + 1) * piece] = jnp.dot(
            tile_ref[pl.ds(start, piece)], grad, preferred_element_type=F32
        ).astype(out_ref.dtype)


def backward_first(chips, tile_ref, *refs):
    *grads, send_ref, bias_ref, grad_ref = refs
    block = grads[0].shape[0]
    z = lax.axis_index("src")
    grads = dict(zip((0, *GRAD), grads))
    for m, piece in grads.items():
        grad_ref[pl.ds(pl.multiple_of((z ^ m) * block, 16), block)] = piece[...]
    rows = [
        jnp.sum(grads[m][...].astype(F32), axis=0, keepdims=True) for m in range(len(grads))
    ]
    tail = split_row(tree(rows))
    bias_ref[...] = jnp.broadcast_to(join_row(tail), bias_ref.shape)
    piece = (send_ref.shape[0] - TAIL) // len(FIRST)
    send_ref[pl.ds(piece * len(FIRST), TAIL)] = tail
    other = 1 - lax.rem(lax.axis_index("dst"), 2)
    half_gradient(other, FIRST, chips, tile_ref, grad_ref[...], send_ref, piece)


def backward_rest(chips, tile_ref, grad_ref, send_ref):
    other = 1 - lax.rem(lax.axis_index("dst"), 2)
    piece = send_ref.shape[0] // len(REST)
    half_gradient(other, REST, chips, tile_ref, grad_ref[...], send_ref, piece)


def backward_keep(chips, tile_ref, grad_ref, keep_ref):
    core = lax.rem(lax.axis_index("dst"), 2)
    piece = keep_ref.shape[0] // chips
    half_gradient(core, range(chips), chips, tile_ref, grad_ref[...], keep_ref, piece)


def add_first(keep_ref, bias_ref, received_ref, total_ref, *sends):
    piece = sends[0].shape[0] - TAIL
    tail = split_row(bias_ref[0:1] + join_row(received_ref[pl.ds(piece * len(FIRST), TAIL)]))
    total_ref[...] = jnp.broadcast_to(join_row(tail), total_ref.shape)
    for i, m in enumerate(FIRST):
        both = keep_ref[pl.ds(m * piece, piece)]
        both = both + received_ref[pl.ds(i * piece, piece)].astype(F32)
        sends[i][0:piece] = both.astype(BF)
        sends[i][piece : piece + TAIL] = tail


def add_rest(keep_ref, total_ref, received_ref, own_ref, *sends):
    piece = own_ref.shape[0]
    for i, m in enumerate(REST):
        both = keep_ref[pl.ds(m * piece, piece)]
        both = both + received_ref[pl.ds(i * piece, piece)].astype(F32)
        if m == 0:
            own_ref[...] = both
        else:
            sends[i][0:piece] = both.astype(BF)
            sends[i][piece : piece + TAIL] = split_row(total_ref[0:1])


def add_chips(own_ref, bias_ref, *refs):
    *received, sum_ref, total_ref = refs
    received = [received[SUMS.index(m)] for m in range(1, len(received) + 1)]
    piece = own_ref.shape[0]
    tails = [join_row(other[pl.ds(piece, TAIL)]) for other in received]
    total_ref[...] = jnp.broadcast_to(tree([bias_ref[0:1]] + tails), total_ref.shape)
    parts = [other[0:piece].astype(F32) for other in received]
    sum_ref[...] = tree([own_ref[...]] + parts).astype(BF)


def add_bands(*refs):
    *parts, out_ref = refs
    out_ref[...] = tree([part[...].astype(F32) for part in parts]).astype(BF)


def spread(which, chunks, out_ref, wide, sems, copies=()):
    me = lax.axis_index("dst")
    rows = chunks[0].shape[0]
    copies = list(copies)
    half = out_ref.shape[0] // 2
    for i, (core, chip) in enumerate(which):
        wide[i] = chunks[i][...].astype(F32)
        start = (lax.rem(me, 2) ^ core) * half + (lax.div(me, 2) ^ chip) * rows
        target = out_ref.at[pl.ds(pl.multiple_of(start, 16), rows)]
        copies.append(pltpu.make_async_copy(wide.at[i], target, sems.at[i]))
        copies[-1].start()
    for copy in copies:
        copy.wait()


def spread_first(which, bias_ref, pre_ref, *refs):
    *chunks, out_ref, row_ref, output_ref, wide, active, row, sems = refs
    row[...] = bias_ref[0:1]
    pre = pre_ref[...]
    active[...] = (pre * jax.nn.sigmoid(pre)).astype(BF)
    copies = [
        pltpu.make_async_copy(row, row_ref, sems.at[len(which)]),
        pltpu.make_async_copy(active, output_ref, sems.at[len(which) + 1]),
    ]
    for copy in copies:
        copy.start()
    spread(which, chunks, out_ref, wide, sems, copies)


def spread_last(which, *refs):
    *chunks, _, out_ref, wide, sems = refs
    spread(which, chunks, out_ref, wide, sems)


def swap(x, axis, n, mask):
    return lax.ppermute(x, axis, [(i, i ^ mask) for i in range(n)])


def on_device(features, relation_weight, bias, block_values, block_list, block_count, cotangent):
    n_dst, n_src = lax.axis_size("dst"), lax.axis_size("src")
    own_rows, width = features.shape
    relations, hidden = relation_weight.shape[1:]
    block_size = block_values.shape[5]
    tile_columns = own_rows * n_dst
    block = cotangent.shape[0]
    band_rows = block * n_src
    few = n_dst == 8 and n_src == 4 and (relations * width) % (8 * 16) == 0
    weight = relation_weight.transpose(1, 0, 2).reshape(relations * width, hidden)
    dense, zero = call(
        functools.partial(assemble, band_rows),
        [shape((relations * band_rows, tile_columns), BF), shape(features.shape, BF)],
        (SMEM, SMEM, VMEM),
        block_list.reshape(relations, -1),
        block_count.reshape(-1),
        block_values.reshape(-1, block_size, block_size),
        flops=10**8,
        moved=4 * 2**20,
    )
    if few:
        return few_devices(features, weight, bias, dense, zero, cotangent, relations)
    gathered = lax.all_gather(features, "dst", axis=0, tiled=True)
    tile = jnp.dot(dense, gathered, preferred_element_type=F32).astype(BF)
    tile = tile.reshape(relations, band_rows, width)
    partial = jnp.einsum(
        "rnd,rdh->nh",
        tile,
        weight.reshape(relations, width, hidden),
        preferred_element_type=F32,
    )
    pre = lax.psum_scatter(partial, "src", scatter_dimension=0, tiled=True)
    pre = pre + bias.astype(F32)
    sigma = jax.nn.sigmoid(pre)
    output = (pre * sigma).astype(BF)
    grad = (cotangent.astype(F32) * sigma * (1.0 + pre * (1.0 - sigma))).astype(BF)
    band_grad = lax.all_gather(grad, "src", axis=0, tiled=True)
    weight_term = jnp.einsum("rnd,nh->rdh", tile, band_grad, preferred_element_type=F32)
    weight_grad, bias_grad = lax.psum(
        (weight_term, jnp.sum(grad.astype(F32), axis=0)), ("dst", "src")
    )
    return output, weight_grad.transpose(1, 0, 2), bias_grad


def few_devices(features, weight, bias, dense, zero, cotangent, relations):
    n_dst, n_src = lax.axis_size("dst"), lax.axis_size("src")
    chips = n_dst // 2
    own_rows, width = features.shape
    block, hidden = cotangent.shape
    band_rows = block * n_src
    total_rows = weight.shape[0]
    piece = total_rows // n_dst
    half = n_dst // 2

    def over_chips(x, m):
        return swap(x, "dst", n_dst, 2 * m)

    def over_core(x):
        return swap(x, "dst", n_dst, 1)

    def over_src(x, m):
        return swap(x, "src", n_src, m)

    near = [features] + [over_chips(features, m) for m in range(1, chips)]
    near[1] = near[1] + zero
    far = [over_core(x) for x in near]
    pieces = [x for pair in zip(near, far) for x in pair]
    half = n_dst // 2
    half_shape = shape((own_rows * half, width), BF)
    message_near, features_near = call(
        forward_near,
        [shape((band_rows, hidden), F32), half_shape],
        [VMEM] * (2 + half),
        dense,
        weight,
        *pieces[:half],
        flops=10**9,
        moved=2**20,
    )
    features_far, own, *sends = call(
        functools.partial(forward, half),
        [half_shape, shape((block, hidden), F32)] + [shape((block, hidden), BF)] * (n_src - 1),
        [VMEM] * (3 + half),
        dense,
        weight,
        message_near,
        *[x for m in FAR for x in (near[m], far[m])],
        scratch=[pltpu.VMEM((band_rows, hidden), F32)],
        flops=10**9,
        moved=2**20,
    )
    received = [over_src(x, m + 1) for m, x in enumerate(sends)]
    turned = call(
        functools.partial(tile_turned, half),
        shape((total_rows, band_rows), BF),
        [VMEM] * 3,
        dense,
        features_near,
        features_far,
        scratch=[pltpu.VMEM((own_rows * n_dst, width), BF)],
        flops=2 * 10**9,
        moved=4 * 2**20,
    )
    pre, grad = call(
        activate,
        [shape((block, hidden), F32), shape((block, hidden), BF)],
        [VMEM] * (2 + n_src),
        bias.reshape(1, hidden),
        cotangent,
        own,
        *[received[m - 1] for m in MESSAGE],
    )
    first, bias_part, band_grad = call(
        functools.partial(backward_first, chips),
        [
            shape((piece * len(FIRST) + TAIL, hidden), BF),
            shape((8, hidden), F32),
            shape((band_rows, hidden), BF),
        ],
        [VMEM] * (1 + n_src),
        turned,
        grad,
        *[over_src(grad, m) for m in GRAD],
    )
    rest = call(
        functools.partial(backward_rest, chips),
        shape((piece * len(REST), hidden), BF),
        [VMEM] * 2,
        turned,
        band_grad,
        flops=3 * 10**8,
        moved=2**20,
    )
    keep = call(
        functools.partial(backward_keep, chips),
        shape((piece * chips, hidden), F32),
        [VMEM] * 2,
        turned,
        band_grad,
        flops=3 * 10**8,
        moved=2**20,
    )
    sent = shape((piece + TAIL, hidden), BF)
    bias_part, *sends = call(
        add_first,
        [shape((8, hidden), F32)] + [sent] * len(FIRST),
        [VMEM] * 3,
        keep,
        bias_part,
        over_core(first),
    )
    own, *others = call(
        add_rest,
        [shape((piece, hidden), F32)] + [sent] * (len(REST) - 1),
        [VMEM] * 3,
        keep,
        bias_part,
        over_core(rest),
    )
    sends = dict(zip(FIRST, sends)) | dict(zip(REST, others))
    received = {m: over_chips(x, m) for m, x in sends.items()}
    part, bias_sum = call(
        add_chips,
        [shape((piece, hidden), BF), shape((8, hidden), F32)],
        [VMEM] * (1 + chips),
        own,
        bias_part,
        *[received[m] for m in SUMS],
    )
    chunk = part
    for m in (1, 3):
        chunk = call(
            add_bands, shape((piece, hidden), BF), [VMEM] * 2, chunk, over_src(chunk, m)
        )
    near = [chunk] + [over_chips(chunk, m) for m in range(1, chips)]
    far = [over_core(x) for x in near]
    chunks = {(0, m): x for m, x in enumerate(near)} | {(1, m): x for m, x in enumerate(far)}
    last = [(0, CHUNKS[-1]), (1, CHUNKS[-1])]
    first = [(core, m) for core in range(2) for m in (0, *CHUNKS[:-1])]
    whole = shape((total_rows, hidden), F32)

    weight_grad, bias_grad, output = call(
        functools.partial(spread_first, first),
        [whole, shape((1, hidden), F32), shape((block, hidden), BF)],
        [VMEM] * (2 + len(first)),
        bias_sum,
        pre,
        *[chunks[w] for w in first],
        scratch=[
            pltpu.VMEM((len(first), piece, hidden), F32),
            pltpu.VMEM((block, hidden), BF),
            pltpu.VMEM((1, hidden), F32),
            pltpu.SemaphoreType.DMA((len(first) + 2,)),
        ],
        out_specs=[ANY] * 3,
    )
    weight_grad = call(
        functools.partial(spread_last, last),
        whole,
        [VMEM] * len(last) + [ANY],
        *[chunks[w] for w in last],
        weight_grad,
        scratch=[
            pltpu.VMEM((len(last), piece, hidden), F32),
            pltpu.SemaphoreType.DMA((len(last),)),
        ],
        aliases={len(last): 0},
        out_specs=ANY,
    )
    weight_grad = weight_grad.reshape(relations, width, hidden).transpose(1, 0, 2)
    return output, weight_grad, bias_grad.reshape(hidden)


def solution(mesh):
    in_specs = (
        P(("src", "dst"), None),
        P(),
        P(),
        P("dst", "src", None, None, None, None),
        P("dst", "src", None, None),
        P("dst", "src", None),
        P(("dst", "src"), None),
    )
    out_specs = (P(("dst", "src"), None), P(), P())
    return jax.shard_map(
        on_device, mesh=mesh, in_specs=in_specs, out_specs=out_specs, check_vma=False
    )
```
